32 devices in a mesh: branch: 4 (over z), dp: 8 (over y, x, core).
Axes of the slice: x: 2, y: 2, z: 4, core: 2. Of those that a mesh axis runs over, the one named last changes fastest.
Arguments:
- tokens: bfloat16 [64, 4096], P('dp'), may hold values from -6 to 6
- routes: int32 [64, 2], P('dp'), may hold values from 0 to 3, all different within a row; in each aligned block of 8 rows (0 to 7, 8 to 15, ...) at most 8 rows name the same one
- route_weights: float32 [64, 2], P('dp'), may hold values from 0.2 to 1
- norm_gains: float32 [4, 4096], P('branch'), may hold values from 0.25 to 1.75
- keyval_weights: bfloat16 [4, 4096, 2048], P('branch', 'dp'), may hold values from -0.09375 to 0.09375
- expert_gate: bfloat16 [4, 4096, 8192], P('branch', None, 'dp'), may hold values from -0.09375 to 0.09375
- expert_up: bfloat16 [4, 4096, 8192], P('branch', None, 'dp'), may hold values from -0.09375 to 0.09375
- expert_down: bfloat16 [4, 8192, 4096], P('branch', None, 'dp'), may hold values from -0.0625 to 0.0625
Outputs:
- mixed: bfloat16 [64, 4096], P('dp')
- merged_keyval: bfloat16 [4096, 2048], P('dp', 'branch')
The draws below stay inside these ranges and needn't reach their ends.
Inputs may be any that keep to these rules, and one draw needn't show every extreme that they name: `routes`: each token names 2 different experts. Among the 8 tokens of one dp index at most 8 name one expert, a bound that some block reaches.
All inputs are finite; a program needn't handle non-finite values.
Results may differ from the reference program's by a relative error of at most 0.013.
Values may be sent and summed in bfloat16 or wider, within the bound.
A program may use at most 64 MiB of HBM per device.

```python
import math
import jax
import jax.numpy as jnp
import numpy as np
from jax import lax

D = 4096
FFW = 8192
KVD = 1024
TOP = 2
TOK_DEV = 8
EXPERTS = 4
CAP = 8
TOKENS = 64
N_DP = 8


def block_scale(key, shape, cuts, low, top_value):
    level, own = 1.0, jax.random.fold_in(key, 6)
    for position, shards_of in cuts:
        heights = jnp.exp(jax.random.uniform(jax.random.fold_in(own, position), (shards_of,), jnp.float32, low / len(cuts), top_value / len(cuts)))
        level = level * jnp.repeat(heights, shape[position] // shards_of).reshape([-1 if axis == position else 1 for axis in range(len(shape))])
    return level


def assign_block(stream_key, own, number, rows, amount, top, most, skew):
    order = jax.random.permutation(stream_key, amount)
    crowded, usual = load_shares(amount, rows * top, most, skew, True), load_shares(amount, rows * top, most, skew, False)
    places = jnp.arange(amount)

    def named(tallies, offset_by):
        used = int((tallies > 0).sum())
        fixed = max(1, used // 4)
        shifted = fixed + (places - fixed + offset_by * (used - fixed)) % max(1, amount - fixed)
        return jnp.zeros((amount,), jnp.int32).at[order[jnp.where(places < fixed, places, shifted)]].set(jnp.asarray(tallies, jnp.int32))

    tallies = jnp.where(number % 4 == 0, named(crowded, number // 4), named(usual, number - number // 4 - 1))
    mixed = jax.random.permutation(jax.random.fold_in(own, 3), amount)
    donor, sink = mixed[0:amount // 2 * 2:2], mixed[1:amount // 2 * 2:2]
    slack = jnp.minimum(tallies[donor] - 1, most - tallies[sink]) // 2
    slack = jnp.where((donor == order[0]) | (sink == order[0]) | (tallies[sink] == 0), 0, jnp.maximum(slack, 0))
    shifted = jax.random.randint(jax.random.fold_in(own, 4), (amount // 2,), 0, 1 << 20) % (slack + 1)
    tallies = tallies.at[donor].add(-shifted).at[sink].add(shifted)
    labels = jnp.searchsorted(jnp.cumsum(tallies), jnp.arange(rows * top), side="right").astype(jnp.int32)
    table = labels.reshape(top, rows).T
    table = table[jax.random.permutation(jax.random.fold_in(own, 1), rows)]
    offset_by = jax.random.randint(jax.random.fold_in(own, 2), (rows, 1), 0, top)
    return jnp.take_along_axis(table, (jnp.arange(top)[None, :] + offset_by) % top, axis=1)


def load_shares(number_of, total, most, lean, full):
    loads = [(1 << 20) // math.isqrt(rank ** lean) + 1 for rank in range(1, number_of + 1)]
    largest = most if full else min(most, max(-(-total // number_of), total * loads[0] // sum(loads)))
    least = 1 if total - largest >= number_of - 1 else 0
    counts, surplus = [largest] + [least] * (number_of - 1), total - largest - least * (number_of - 1)
    while surplus > 0:
        movable = [i for i in range(1, number_of) if counts[i] < largest] or [i for i in range(1, number_of) if counts[i] < most]
        mass, remaining = sum([loads[i] for i in movable]), surplus
        for i in movable:
            more = min(most - counts[i], max(1, remaining * loads[i] // mass), surplus)
            counts[i] = counts[i] + more
            surplus = surplus - more
    return np.array(counts)


def bell_draw(key, extent, scale, bound, cuts=(), kind=jnp.bfloat16):
    loudness = block_scale(key, extent, cuts, -0.22, 0.18) if cuts else 1.0
    values = jax.random.normal(key, extent, jnp.float32) * scale * loudness
    return jnp.minimum(jnp.maximum(values, -bound), bound).astype(kind)


def setup_inputs(seed: int = 0) -> dict:
    seeds = jax.random.split(jax.random.key(seed), 9)
    tokens = bell_draw(seeds[0], (TOKENS, D), 1.0, 6.0, ((0, 8),))
    routes_keys = jax.random.split(jax.random.fold_in(seeds[1], 1), TOKENS // TOK_DEV)
    routes_turns = jax.random.permutation(jax.random.fold_in(seeds[1], 3), TOKENS // TOK_DEV)
    routes = jax.vmap(lambda own, number: assign_block(jax.random.fold_in(seeds[1], 2), own, number, TOK_DEV, EXPERTS, TOP, CAP, 2))(routes_keys, routes_turns).reshape((TOKENS, TOP))
    route_weights = jnp.clip(0.2 + 0.8 * jax.random.uniform(seeds[2], (TOKENS, TOP), jnp.float32) ** block_scale(seeds[2], (TOKENS, TOP), ((0, 8),), -0.2, 0.2), 0.2, 1.0)
    norm_gains = jnp.clip(1.0 + 0.15 * jax.random.normal(seeds[3], (EXPERTS, D), jnp.float32), 0.25, 1.75)
    keyval_weights = bell_draw(seeds[4], (EXPERTS, D, 2 * KVD), D ** -0.5, 0.09375, ((0, 4), (1, 8)))
    expert_gate = bell_draw(seeds[5], (EXPERTS, D, FFW), D ** -0.5, 0.09375, ((0, 4), (2, 8)))
    expert_up = bell_draw(seeds[6], (EXPERTS, D, FFW), D ** -0.5, 0.09375, ((0, 4), (2, 8)))
    expert_down = bell_draw(seeds[7], (EXPERTS, FFW, D), FFW ** -0.5, 0.0625, ((0, 4), (2, 8)))
    return dict(tokens=tokens, routes=routes, route_weights=route_weights, norm_gains=norm_gains, keyval_weights=keyval_weights, expert_gate=expert_gate, expert_up=expert_up, expert_down=expert_down)


def reference(tokens, routes, route_weights, norm_gains, keyval_weights, expert_gate, expert_up, expert_down):
    gain_avg = lax.optimization_barrier(jnp.mean(norm_gains, axis=0))
    merged_keyval = lax.optimization_barrier(jnp.mean(keyval_weights.astype(jnp.float32), axis=0)).astype(jnp.bfloat16)
    widened = tokens.astype(jnp.float32)
    inv_rms = lax.rsqrt(lax.optimization_barrier(jnp.mean(widened * widened, axis=1, keepdims=True)) + 1e-05)
    normed = (widened * inv_rms * gain_avg[None, :]).astype(jnp.bfloat16)
    capacity = min(TOK_DEV, 4 * TOK_DEV // EXPERTS)
    shard_rows = normed.astype(jnp.float32).reshape(N_DP, TOK_DEV, D)
    route_shards = routes.reshape(N_DP, TOK_DEV, TOP)
    weight_shards = route_weights.reshape(N_DP, TOK_DEV, TOP)
    running = jnp.zeros((N_DP, TOK_DEV, D), jnp.float32)
    for expert in range(EXPERTS):
        matched = route_shards == expert
        chosen = jnp.any(matched, axis=2)
        weight_share = lax.optimization_barrier(jnp.sum(jnp.where(matched, weight_shards, jnp.zeros_like(weight_shards)), axis=2))
        slot_index = jnp.cumsum(chosen.astype(jnp.int32), axis=1) - 1
        picks = ((slot_index[:, None, :] == jnp.arange(capacity, dtype=jnp.int32)[None, :, None]) & chosen[:, None, :]).astype(jnp.float32)
        packed = jnp.einsum('nct,ntd->ncd', picks, shard_rows).astype(jnp.bfloat16).reshape(N_DP * capacity, D)
        gate_part = jnp.dot(packed, expert_gate[expert], preferred_element_type=jnp.float32)
        up_part = jnp.dot(packed, expert_up[expert], preferred_element_type=jnp.float32)
        hidden = (jax.nn.silu(gate_part) * up_part).astype(jnp.bfloat16)
        result = jnp.dot(hidden, expert_down[expert], preferred_element_type=jnp.float32).astype(jnp.bfloat16)
        returned = jnp.einsum('nct,ncd->ntd', picks, result.astype(jnp.float32).reshape(N_DP, capacity, D))
        running = running + returned * weight_share[:, :, None]
    mixed = (widened + running.reshape(TOKENS, D)).astype(jnp.bfloat16)
    return (mixed, merged_keyval)
```

```python
import functools

import jax
import jax.numpy as jnp
from jax import lax
from jax.experimental import pallas as pl
from jax.experimental.pallas import tpu as pltpu
from jax.sharding import PartitionSpec as P

MESH = pl.DeviceIdType.MESH
CHUNKS = 2


def kernel(
    B,
    N,
    tokens,
    routes,
    route_weights,
    gains,
    keyval,
    gate,
    up,
    down,
    moe_out,
    kv_out,
    tg,
    gg,
    normed,
    wg,
    wu,
    wd,
    kv,
    flow,
    hid,
    acc,
    rs,
    ret,
    part,
    tok_s,
    tok_r,
    gain_s,
    gain_r,
    hid_s,
    hid_r,
    ret_s,
    ret_r,
    part_s,
    part_r,
    kv_s,
    kv_r,
    wg_sem,
    wu_sem,
    wd_sem,
    kv_sem,
):
    b, me = lax.axis_index("branch"), lax.axis_index("dp")
    T, D = tokens.shape
    R = N * T
    C, _, ct = hid.shape[1], hid.shape[2], hid.shape[3]
    rows, bw = kv_out.shape
    crows = rows // CHUNKS
    F = C * ct

    def dp_peer(k):
        return lax.rem(me + k, N)

    def br_peer(k):
        return lax.rem(b + k, B)

    load_kv = pltpu.make_async_copy(keyval.at[0], kv, kv_sem)
    load_kv.start()
    loads = []
    for c in range(C):
        cols = pl.ds(c * ct, ct)
        one = pltpu.make_async_copy(gate.at[0, :, cols], wg.at[c], wg_sem.at[c])
        two = pltpu.make_async_copy(up.at[0, :, cols], wu.at[c], wu_sem.at[c])
        one.start()
        two.start()
        loads.append((one, two))
    load_wd = pltpu.make_async_copy(down.at[0], wd, wd_sem)
    load_wd.start()

    barrier = pltpu.get_barrier_semaphore()

    @pl.loop(1, N)
    def _(k):
        pl.semaphore_signal(barrier, inc=1, device_id={"dp": dp_peer(k)}, device_id_type=MESH)

    @pl.loop(1, B)
    def _(k):
        pl.semaphore_signal(barrier, inc=1, device_id={"branch": br_peer(k)}, device_id_type=MESH)

    tg[me] = tokens[...]
    gg[b] = gains[...]
    pl.semaphore_wait(barrier, N - 1 + B - 1)

    def dp_copy(src, dst, ss, rsm, peer):
        return pltpu.make_async_remote_copy(
            src_ref=src, dst_ref=dst, send_sem=ss, recv_sem=rsm,
            device_id={"dp": peer}, device_id_type=MESH,
        )

    def br_copy(src, dst, ss, rsm, peer):
        return pltpu.make_async_remote_copy(
            src_ref=src, dst_ref=dst, send_sem=ss, recv_sem=rsm,
            device_id={"branch": peer}, device_id_type=MESH,
        )

    def gain_copy(slot, peer):
        return br_copy(gg.at[slot], gg.at[slot], gain_s.at[peer], gain_r.at[slot], peer)

    def tok_copy(slot, peer):
        return dp_copy(tg.at[slot], tg.at[slot], tok_s.at[peer], tok_r.at[slot], peer)

    @pl.loop(1, B)
    def _(k):
        gain_copy(b, br_peer(k)).start()

    @pl.loop(1, N)
    def _(k):
        tok_copy(me, dp_peer(k)).start()

    steps = CHUNKS * (B - 1)
    place = (b, B - 1 - b)

    def target(way, s):
        far = B - 1 - s // CHUNKS
        return far, (far if way == 0 else B - 1 - far)

    def kv_copy(way, d, c):
        to = jnp.clip(b + 1 if way == 0 else b - 1, 0, B - 1)
        slot = flow.at[way, d, c]
        return br_copy(slot, slot, kv_s.at[way, d, c], kv_r.at[way, d, c], to)

    def own(d, c):
        return kv[pl.ds(c * crows, crows), pl.ds(pl.multiple_of(d * bw, bw), bw)]

    def step(way, s):
        at = place[way]
        far, d = target(way, s)
        c = lax.rem(s, CHUNKS)

        @pl.when((s >= 0) & (s < steps) & (far > at))
        def _():
            mine = kv[
                pl.ds(pl.multiple_of(c * crows, crows), crows),
                pl.ds(pl.multiple_of(d * bw, bw), bw),
            ]

            @pl.when(at == 0)
            def _():
                flow[way, d, c] = mine

            @pl.when(at > 0)
            def _():
                kv_copy(way, d, c).wait_recv()
                flow[way, d, c] = (
                    flow[way, d, c].astype(jnp.float32) + mine.astype(jnp.float32)
                ).astype(jnp.bfloat16)

            kv_copy(way, d, c).start()

    def sent(way, s):
        far, d = target(way, s)
        c = lax.rem(s, CHUNKS)

        @pl.when((s >= 0) & (s < steps) & (far > place[way]))
        def _():
            kv_copy(way, d, c).wait_send()

    def slot(p):
        for way in range(2):
            s = jnp.where(place[way] == 0, p + 1, p - place[way])
            sent(way, s - 2)
            step(way, s)

    load_kv.wait()
    slot(jnp.int32(-1))
    slot(jnp.int32(0))

    @pl.loop(1, B)
    def _(k):
        gain_copy(br_peer(k), br_peer(k)).wait_recv()

    gain = gg[0]
    for e in range(1, B):
        gain = gain + gg[e]
    gain = gain / B
    gg_avg = gain

    @pl.loop(1, N)
    def _(k):
        tok_copy(dp_peer(k), dp_peer(k)).wait_recv()

    pair = 2

    @pl.loop(0, N // pair)
    def _(i):
        x = jnp.concatenate([tg[i * pair + q].astype(jnp.float32) for q in range(pair)], axis=0)
        inv = lax.rsqrt(jnp.mean(x * x, axis=1, keepdims=True) + 1e-05)
        normed[pl.ds(pl.multiple_of(i * pair * T, pair * T), pair * T), :] = (
            x * inv * gg_avg
        ).astype(jnp.bfloat16)

    def hid_copy(c, slot_, peer):
        return dp_copy(
            hid.at[slot_, c], hid.at[slot_, c], hid_s.at[c, peer], hid_r.at[c, slot_], peer
        )

    for c in range(C):
        loads[c][0].wait()
        loads[c][1].wait()
        x = normed[...]
        g = jnp.dot(x, wg[c], preferred_element_type=jnp.float32)
        u = jnp.dot(x, wu[c], preferred_element_type=jnp.float32)
        hid[me, c] = (g / (1.0 + jnp.exp(-g)) * u).astype(jnp.bfloat16)

        @pl.loop(1, N)
        def _(k, c=c):
            hid_copy(c, me, dp_peer(k)).start()

    slot(jnp.int32(1))

    load_wd.wait()
    acc[...] = jnp.zeros_like(acc)
    for c in range(C):

        @pl.loop(0, N)
        def _(k, c=c):
            j = dp_peer(k)

            @pl.when(k > 0)
            def _():
                hid_copy(c, j, j).wait_recv()

            acc[...] += jnp.dot(
                hid[j, c],
                wd[pl.ds(pl.multiple_of(j * F + c * ct, ct), ct), :],
                preferred_element_type=jnp.float32,
            )

    slot(jnp.int32(2))

    def ret_copy(i, peer, from_):
        return dp_copy(rs.at[i], ret.at[from_], ret_s.at[i], ret_r.at[from_], peer)

    @pl.loop(0, N)
    def _(i):
        rs[i] = acc[pl.ds(pl.multiple_of(i * T, T), T), :].astype(jnp.bfloat16)

    @pl.loop(1, N)
    def _(k):
        ret_copy(dp_peer(k), dp_peer(k), me).start()

    ret[me] = rs[me]
    weight = jnp.sum(
        jnp.where(routes[...] == b, route_weights[...], 0.0), axis=1, keepdims=True
    )

    @pl.loop(0, N)
    def _(k):
        j = dp_peer(k)

        @pl.when(k > 0)
        def _():
            ret_copy(j, j, j).wait_recv()

        part[b, j] = (ret[j].astype(jnp.float32) * weight).astype(jnp.bfloat16)

    def part_copy(e, peer):
        return br_copy(part.at[e], part.at[e], part_s.at[peer], part_r.at[e], peer)

    @pl.loop(1, B)
    def _(k):
        part_copy(b, br_peer(k)).start()

    slot(jnp.int32(3))

    @pl.loop(1, B)
    def _(k):
        part_copy(br_peer(k), br_peer(k)).wait_recv()

    @pl.loop(0, N)
    def _(j):
        total = part[0, j].astype(jnp.float32)
        for e in range(1, B):
            total = total + part[e, j].astype(jnp.float32)
        moe_out[j] = total

    @pl.loop(4, steps + B)
    def _(p):
        slot(p)

    for way in range(2):

        @pl.when(place[way] == 0)
        def _(way=way):
            flow[way, b] = jnp.zeros_like(flow[way, b])

        @pl.when(place[way] > 0)
        def _(way=way):
            for c in range(CHUNKS):
                kv_copy(way, b, c).wait_recv()

    for c in range(CHUNKS):
        total = (
            own(b, c).astype(jnp.float32)
            + flow[0, b, c].astype(jnp.float32)
            + flow[1, b, c].astype(jnp.float32)
        )
        kv_out[pl.ds(c * crows, crows), :] = (total / B).astype(jnp.bfloat16)

    for way in range(2):
        last = jnp.where(place[way] == 0, steps + B, steps + B - 1 - place[way])

        @pl.loop(0, steps)
        def _(s, way=way, last=last):
            @pl.when(s > last - 2)
            def _():
                sent(way, s)

    @pl.loop(1, B)
    def _(k):
        gain_copy(b, br_peer(k)).wait_send()
        part_copy(b, br_peer(k)).wait_send()

    @pl.loop(1, N)
    def _(k):
        tok_copy(me, dp_peer(k)).wait_send()
        ret_copy(dp_peer(k), dp_peer(k), me).wait_send()
        for c in range(C):
            hid_copy(c, me, dp_peer(k)).wait_send()


def local(tokens, routes, route_weights, norm_gains, keyval, gate, up, down):
    B, N = lax.axis_size("branch"), lax.axis_size("dp")
    T, D = tokens.shape
    F = gate.shape[2]
    ct = min(256, F)
    C = F // ct
    rows, wide = keyval.shape[1:]
    bw = wide // B
    H, bc = down.shape[1:]
    bf, f32 = jnp.bfloat16, jnp.float32
    dma = pltpu.SemaphoreType.DMA
    vmem, anys = pl.BlockSpec(memory_space=pltpu.VMEM), pl.BlockSpec(memory_space=pl.ANY)
    moe, merged = pl.pallas_call(
        functools.partial(kernel, B, N),
        out_shape=(
            jax.ShapeDtypeStruct((N, T, bc), f32),
            jax.ShapeDtypeStruct((rows, bw), bf),
        ),
        in_specs=[vmem] * 4 + [anys] * 4,
        out_specs=(vmem, vmem),
        scratch_shapes=[
            pltpu.VMEM((N, T, D), bf),
            pltpu.VMEM((B, 1, D), f32),
            pltpu.VMEM((N * T, D), bf),
            pltpu.VMEM((C, D, ct), bf),
            pltpu.VMEM((C, D, ct), bf),
            pltpu.VMEM((H, bc), bf),
            pltpu.VMEM((rows, wide), bf),
            pltpu.VMEM((2, B, CHUNKS, rows // CHUNKS, bw), bf),
            pltpu.VMEM((N, C, N * T, ct), bf),
            pltpu.VMEM((N * T, bc), f32),
            pltpu.VMEM((N, T, bc), bf),
            pltpu.VMEM((N, T, bc), bf),
            pltpu.VMEM((B, N, T, bc), bf),
            dma((N,)),
            dma((N,)),
            dma((B,)),
            dma((B,)),
            dma((C, N)),
            dma((C, N)),
            dma((N,)),
            dma((N,)),
            dma((B,)),
            dma((B,)),
            dma((2, B, CHUNKS)),
            dma((2, B, CHUNKS)),
            dma((C,)),
            dma((C,)),
            dma,
            dma,
        ],
        compiler_params=pltpu.CompilerParams(
            collective_id=0, has_side_effects=True, vmem_limit_bytes=56 * 2**20
        ),
    )(tokens, routes, route_weights, norm_gains, keyval, gate, up, down)
    moe = jnp.transpose(moe, (1, 0, 2)).reshape(T, D)
    return (tokens.astype(f32) + moe).astype(bf), merged


def solution(mesh):
    in_specs = (
        P("dp", None),
        P("dp", None),
        P("dp", None),
        P("branch", None),
        P("branch", "dp", None),
        P("branch", None, "dp"),
        P("branch", None, "dp"),
        P("branch", None, "dp"),
    )
    out_specs = (P("dp", None), P("dp", "branch"))
    return jax.shard_map(local, mesh=mesh, in_specs=in_specs, out_specs=out_specs, check_vma=False)
```

```python
import functools

import jax
import jax.numpy as jnp
from jax import lax
from jax.experimental import pallas as pl
from jax.experimental.pallas import tpu as pltpu
from jax.sharding import PartitionSpec as P

MESH = pl.DeviceIdType.MESH
CHUNKS = 2


def kernel(
    B,
    N,
    tokens,
    routes,
    route_weights,
    gains,
    keyval,
    gate,
    up,
    down,
    moe_out,
    kv_out,
    tg,
    gg,
    normed,
    wg,
    wu,
    wd,
    kv,
    flow,
    hid,
    acc,
    rs,
    ret,
    part,
    tok_s,
    tok_r,
    gain_s,
    gain_r,
    hid_s,
    hid_r,
    ret_s,
    ret_r,
    part_s,
    part_r,
    kv_s,
    kv_r,
    wg_sem,
    wu_sem,
    wd_sem,
    kv_sem,
):
    b, me = lax.axis_index("branch"), lax.axis_index("dp")
    T, D = tokens.shape
    R = N * T
    C, _, ct = hid.shape[1], hid.shape[2], hid.shape[3]
    rows, bw = kv_out.shape
    crows = rows // CHUNKS
    F = C * ct

    def dp_peer(k):
        return lax.rem(me + k, N)

    def br_peer(k):
        return lax.rem(b + k, B)

    load_kv = pltpu.make_async_copy(keyval.at[0], kv, kv_sem)
    load_kv.start()
    barrier = pltpu.get_barrier_semaphore()

    @pl.loop(1, N)
    def _(k):
        pl.semaphore_signal(barrier, inc=1, device_id={"dp": dp_peer(k)}, device_id_type=MESH)

    @pl.loop(1, B)
    def _(k):
        pl.semaphore_signal(barrier, inc=1, device_id={"branch": br_peer(k)}, device_id_type=MESH)

    tg[me] = tokens[...]
    gg[b] = gains[...]
    pl.semaphore_wait(barrier, N - 1 + B - 1)

    def dp_copy(src, dst, ss, rsm, peer):
        return pltpu.make_async_remote_copy(
            src_ref=src, dst_ref=dst, send_sem=ss, recv_sem=rsm,
            device_id={"dp": peer}, device_id_type=MESH,
        )

    def br_copy(src, dst, ss, rsm, peer):
        return pltpu.make_async_remote_copy(
            src_ref=src, dst_ref=dst, send_sem=ss, recv_sem=rsm,
            device_id={"branch": peer}, device_id_type=MESH,
        )

    def gain_copy(slot, peer):
        return br_copy(gg.at[slot], gg.at[slot], gain_s.at[peer], gain_r.at[slot], peer)

    def tok_copy(slot, peer):
        return dp_copy(tg.at[slot], tg.at[slot], tok_s.at[peer], tok_r.at[slot], peer)

    @pl.loop(1, B)
    def _(k):
        gain_copy(b, br_peer(k)).start()

    @pl.loop(1, N)
    def _(k):
        tok_copy(me, dp_peer(k)).start()

    loads = []
    for c in range(C):
        cols = pl.ds(c * ct, ct)
        one = pltpu.make_async_copy(gate.at[0, :, cols], wg.at[c], wg_sem.at[c])
        two = pltpu.make_async_copy(up.at[0, :, cols], wu.at[c], wu_sem.at[c])
        one.start()
        two.start()
        loads.append((one, two))
    load_wd = pltpu.make_async_copy(down.at[0], wd, wd_sem)
    load_wd.start()

    steps = CHUNKS * (B - 1)
    place = (b, B - 1 - b)

    def target(way, s):
        far = B - 1 - s // CHUNKS
        return far, (far if way == 0 else B - 1 - far)

    def kv_copy(way, d, c):
        to = jnp.clip(b + 1 if way == 0 else b - 1, 0, B - 1)
        slot = flow.at[way, d, c]
        return br_copy(slot, slot, kv_s.at[way, d, c], kv_r.at[way, d, c], to)

    def own(d, c):
        return kv[pl.ds(c * crows, crows), pl.ds(pl.multiple_of(d * bw, bw), bw)]

    def step(way, s):
        at = place[way]
        far, d = target(way, s)
        c = lax.rem(s, CHUNKS)

        @pl.when((s >= 0) & (s < steps) & (far > at))
        def _():
            mine = kv[
                pl.ds(pl.multiple_of(c * crows, crows), crows),
                pl.ds(pl.multiple_of(d * bw, bw), bw),
            ]

            @pl.when(at == 0)
            def _():
                flow[way, d, c] = mine

            @pl.when(at > 0)
            def _():
                kv_copy(way, d, c).wait_recv()
                flow[way, d, c] = (
                    flow[way, d, c].astype(jnp.float32) + mine.astype(jnp.float32)
                ).astype(jnp.bfloat16)

            kv_copy(way, d, c).start()

    def sent(way, s):
        far, d = target(way, s)
        c = lax.rem(s, CHUNKS)

        @pl.when((s >= 0) & (s < steps) & (far > place[way]))
        def _():
            kv_copy(way, d, c).wait_send()

    def slot(p):
        for way in range(2):
            s = jnp.where(place[way] == 0, p + 1, p - place[way])
            sent(way, s - 2)
            step(way, s)

    load_kv.wait()
    slot(jnp.int32(-1))
    slot(jnp.int32(0))

    @pl.loop(1, B)
    def _(k):
        gain_copy(br_peer(k), br_peer(k)).wait_recv()

    gain = gg[0]
    for e in range(1, B):
        gain = gain + gg[e]
    gain = gain / B
    gg_avg = gain

    @pl.loop(1, N)
    def _(k):
        tok_copy(dp_peer(k), dp_peer(k)).wait_recv()

    pair = 2

    @pl.loop(0, N // pair)
    def _(i):
        x = jnp.concatenate([tg[i * pair + q].astype(jnp.float32) for q in range(pair)], axis=0)
        inv = lax.rsqrt(jnp.mean(x * x, axis=1, keepdims=True) + 1e-05)
        normed[pl.ds(pl.multiple_of(i * pair * T, pair * T), pair * T), :] = (
            x * inv * gg_avg
        ).astype(jnp.bfloat16)

    def hid_copy(c, slot_, peer):
        return dp_copy(
            hid.at[slot_, c], hid.at[slot_, c], hid_s.at[c, peer], hid_r.at[c, slot_], peer
        )

    for c in range(C):
        loads[c][0].wait()
        loads[c][1].wait()
        x = normed[...]
        g = jnp.dot(x, wg[c], preferred_element_type=jnp.float32)
        u = jnp.dot(x, wu[c], preferred_element_type=jnp.float32)
        hid[me, c] = (g / (1.0 + jnp.exp(-g)) * u).astype(jnp.bfloat16)

        @pl.loop(1, N)
        def _(k, c=c):
            hid_copy(c, me, dp_peer(k)).start()

        if c == 0:
            slot(jnp.int32(1))
        if c == C - 1:
            slot(jnp.int32(2))

    load_wd.wait()
    acc[...] = jnp.zeros_like(acc)
    for c in range(C):

        @pl.loop(0, N)
        def _(k, c=c):
            j = dp_peer(k)

            @pl.when(k > 0)
            def _():
                hid_copy(c, j, j).wait_recv()

            acc[...] += jnp.dot(
                hid[j, c],
                wd[pl.ds(pl.multiple_of(j * F + c * ct, ct), ct), :],
                preferred_element_type=jnp.float32,
            )

        if c == 0:
            slot(jnp.int32(3))
        if c == C - 1:
            slot(jnp.int32(4))

    def ret_copy(i, peer, from_):
        return dp_copy(rs.at[i], ret.at[from_], ret_s.at[i], ret_r.at[from_], peer)

    @pl.loop(0, N)
    def _(i):
        rs[i] = acc[pl.ds(pl.multiple_of(i * T, T), T), :].astype(jnp.bfloat16)

    @pl.loop(1, N)
    def _(k):
        ret_copy(dp_peer(k), dp_peer(k), me).start()

    ret[me] = rs[me]
    row = jnp.sum(jnp.where(routes[...] == b, route_weights[...], 0.0), axis=0, keepdims=True)
    diagonal = lax.broadcasted_iota(jnp.int32, (T, T), 0) == lax.broadcasted_iota(
        jnp.int32, (T, T), 1
    )
    weight = jnp.sum(jnp.where(diagonal, row, 0.0), axis=1, keepdims=True)

    @pl.loop(0, N)
    def _(k):
        j = dp_peer(k)

        @pl.when(k > 0)
        def _():
            ret_copy(j, j, j).wait_recv()

        part[b, j] = (ret[j].astype(jnp.float32) * weight).astype(jnp.bfloat16)

    def part_copy(e, peer):
        return br_copy(part.at[e], part.at[e], part_s.at[peer], part_r.at[e], peer)

    @pl.loop(1, B)
    def _(k):
        part_copy(b, br_peer(k)).start()

    @pl.loop(1, B)
    def _(k):
        part_copy(br_peer(k), br_peer(k)).wait_recv()

    @pl.loop(0, N)
    def _(j):
        total = part[0, j].astype(jnp.float32)
        for e in range(1, B):
            total = total + part[e, j].astype(jnp.float32)
        moe_out[j] = total

    @pl.loop(5, steps + B)
    def _(p):
        slot(p)

    for way in range(2):

        @pl.when(place[way] == 0)
        def _(way=way):
            flow[way, b] = jnp.zeros_like(flow[way, b])

        @pl.when(place[way] > 0)
        def _(way=way):
            for c in range(CHUNKS):
                kv_copy(way, b, c).wait_recv()

    for c in range(CHUNKS):
        total = (
            own(b, c).astype(jnp.float32)
            + flow[0, b, c].astype(jnp.float32)
            + flow[1, b, c].astype(jnp.float32)
        )
        kv_out[pl.ds(c * crows, crows), :] = (total / B).astype(jnp.bfloat16)

    for way in range(2):
        last = jnp.where(place[way] == 0, steps + B, steps + B - 1 - place[way])

        @pl.loop(0, steps)
        def _(s, way=way, last=last):
            @pl.when(s > last - 2)
            def _():
                sent(way, s)

    @pl.loop(1, B)
    def _(k):
        gain_copy(b, br_peer(k)).wait_send()
        part_copy(b, br_peer(k)).wait_send()

    @pl.loop(1, N)
    def _(k):
        tok_copy(me, dp_peer(k)).wait_send()
        ret_copy(dp_peer(k), dp_peer(k), me).wait_send()
        for c in range(C):
            hid_copy(c, me, dp_peer(k)).wait_send()


def local(tokens, routes, route_weights, norm_gains, keyval, gate, up, down):
    B, N = lax.axis_size("branch"), lax.axis_size("dp")
    T, D = tokens.shape
    F = gate.shape[2]
    ct = min(256, F)
    C = F // ct
    rows, wide = keyval.shape[1:]
    bw = wide // B
    H, bc = down.shape[1:]
    bf, f32 = jnp.bfloat16, jnp.float32
    dma = pltpu.SemaphoreType.DMA
    vmem, anys = pl.BlockSpec(memory_space=pltpu.VMEM), pl.BlockSpec(memory_space=pl.ANY)
    moe, merged = pl.pallas_call(
        functools.partial(kernel, B, N),
        out_shape=(
            jax.ShapeDtypeStruct((N, T, bc), f32),
            jax.ShapeDtypeStruct((rows, bw), bf),
        ),
        in_specs=[vmem] * 4 + [anys] * 4,
        out_specs=(vmem, vmem),
        scratch_shapes=[
            pltpu.VMEM((N, T, D), bf),
            pltpu.VMEM((B, 1, D), f32),
            pltpu.VMEM((N * T, D), bf),
            pltpu.VMEM((C, D, ct), bf),
            pltpu.VMEM((C, D, ct), bf),
            pltpu.VMEM((H, bc), bf),
            pltpu.VMEM((rows, wide), bf),
            pltpu.VMEM((2, B, CHUNKS, rows // CHUNKS, bw), bf),
            pltpu.VMEM((N, C, N * T, ct), bf),
            pltpu.VMEM((N * T, bc), f32),
            pltpu.VMEM((N, T, bc), bf),
            pltpu.VMEM((N, T, bc), bf),
            pltpu.VMEM((B, N, T, bc), bf),
            dma((N,)),
            dma((N,)),
            dma((B,)),
            dma((B,)),
            dma((C, N)),
            dma((C, N)),
            dma((N,)),
            dma((N,)),
            dma((B,)),
            dma((B,)),
            dma((2, B, CHUNKS)),
            dma((2, B, CHUNKS)),
            dma((C,)),
            dma((C,)),
            dma,
            dma,
        ],
        compiler_params=pltpu.CompilerParams(
            collective_id=0, has_side_effects=True, vmem_limit_bytes=56 * 2**20
        ),
    )(tokens, routes.T, route_weights.T, norm_gains, keyval, gate, up, down)
    moe = jnp.transpose(moe, (1, 0, 2)).reshape(T, D)
    return (tokens.astype(f32) + moe).astype(bf), merged


def solution(mesh):
    in_specs = (
        P("dp", None),
        P("dp", None),
        P("dp", None),
        P("branch", None),
        P("branch", "dp", None),
        P("branch", None, "dp"),
        P("branch", None, "dp"),
        P("branch", None, "dp"),
    )
    out_specs = (P("dp", None), P("dp", "branch"))
    return jax.shard_map(local, mesh=mesh, in_specs=in_specs, out_specs=out_specs, check_vma=False)
```

```python
import functools

import jax
import jax.numpy as jnp
from jax import lax
from jax.experimental import pallas as pl
from jax.experimental.pallas import tpu as pltpu
from jax.sharding import PartitionSpec as P

MESH = pl.DeviceIdType.MESH
CHUNKS = 2


def kernel(
    B,
    N,
    tokens,
    routes,
    route_weights,
    gains,
    keyval,
    gate,
    up,
    down,
    moe_out,
    kv_out,
    tg,
    gg,
    normed,
    wg,
    wu,
    wd,
    kv,
    flow,
    hid,
    acc,
    rs,
    ret,
    part,
    tok_s,
    tok_r,
    gain_s,
    gain_r,
    hid_s,
    hid_r,
    ret_s,
    ret_r,
    part_s,
    part_r,
    kv_s,
    kv_r,
    wg_sem,
    wu_sem,
    wd_sem,
    kv_sem,
):
    b, me = lax.axis_index("branch"), lax.axis_index("dp")
    T, D = tokens.shape
    R = N * T
    C, _, ct = hid.shape[1], hid.shape[2], hid.shape[3]
    rows, bw = kv_out.shape
    crows = rows // CHUNKS
    F = C * ct

    def dp_peer(k):
        return lax.rem(me + k, N)

    def br_peer(k):
        return lax.rem(b + k, B)

    load_kv = pltpu.make_async_copy(keyval.at[0], kv, kv_sem)
    load_kv.start()
    barrier = pltpu.get_barrier_semaphore()

    @pl.loop(1, N)
    def _(k):
        pl.semaphore_signal(barrier, inc=1, device_id={"dp": dp_peer(k)}, device_id_type=MESH)

    @pl.loop(1, B)
    def _(k):
        pl.semaphore_signal(barrier, inc=1, device_id={"branch": br_peer(k)}, device_id_type=MESH)

    tg[me] = tokens[...]
    gg[b] = gains[...]
    pl.semaphore_wait(barrier, N - 1 + B - 1)

    def dp_copy(src, dst, ss, rsm, peer):
        return pltpu.make_async_remote_copy(
            src_ref=src, dst_ref=dst, send_sem=ss, recv_sem=rsm,
            device_id={"dp": peer}, device_id_type=MESH,
        )

    def br_copy(src, dst, ss, rsm, peer):
        return pltpu.make_async_remote_copy(
            src_ref=src, dst_ref=dst, send_sem=ss, recv_sem=rsm,
            device_id={"branch": peer}, device_id_type=MESH,
        )

    def gain_copy(slot, peer):
        return br_copy(gg.at[slot], gg.at[slot], gain_s.at[peer], gain_r.at[slot], peer)

    def tok_copy(slot, peer):
        return dp_copy(tg.at[slot], tg.at[slot], tok_s.at[peer], tok_r.at[slot], peer)

    @pl.loop(1, N)
    def _(k):
        tok_copy(me, dp_peer(k)).start()

    @pl.loop(1, B)
    def _(k):
        gain_copy(b, br_peer(k)).start()

    loads = []
    for c in range(C):
        cols = pl.ds(c * ct, ct)
        one = pltpu.make_async_copy(gate.at[0, :, cols], wg.at[c], wg_sem.at[c])
        two = pltpu.make_async_copy(up.at[0, :, cols], wu.at[c], wu_sem.at[c])
        one.start()
        two.start()
        loads.append((one, two))
    load_wd = pltpu.make_async_copy(down.at[0], wd, wd_sem)
    load_wd.start()

    steps = CHUNKS * (B - 1)
    place = (b, B - 1 - b)

    def target(way, s):
        far = B - 1 - s // CHUNKS
        return far, (far if way == 0 else B - 1 - far)

    def kv_copy(way, d, c):
        to = jnp.clip(b + 1 if way == 0 else b - 1, 0, B - 1)
        slot = flow.at[way, d, c]
        return br_copy(slot, slot, kv_s.at[way, d, c], kv_r.at[way, d, c], to)

    def own(d, c):
        return kv[pl.ds(c * crows, crows), pl.ds(pl.multiple_of(d * bw, bw), bw)]

    def step(way, s):
        at = place[way]
        far, d = target(way, s)
        c = lax.rem(s, CHUNKS)

        @pl.when((s >= 0) & (s < steps) & (far > at))
        def _():
            mine = kv[
                pl.ds(pl.multiple_of(c * crows, crows), crows),
                pl.ds(pl.multiple_of(d * bw, bw), bw),
            ]

            @pl.when(at == 0)
            def _():
                flow[way, d, c] = mine

            @pl.when(at > 0)
            def _():
                kv_copy(way, d, c).wait_recv()
                flow[way, d, c] = (
                    flow[way, d, c].astype(jnp.float32) + mine.astype(jnp.float32)
                ).astype(jnp.bfloat16)

            kv_copy(way, d, c).start()

    def sent(way, s):
        far, d = target(way, s)
        c = lax.rem(s, CHUNKS)

        @pl.when((s >= 0) & (s < steps) & (far > place[way]))
        def _():
            kv_copy(way, d, c).wait_send()

    def slot(p):
        for way in range(2):
            s = jnp.where(place[way] == 0, p + 1, p - place[way])
            sent(way, s - 2)
            step(way, s)

    load_kv.wait()
    slot(jnp.int32(-1))
    slot(jnp.int32(0))

    @pl.loop(1, B)
    def _(k):
        gain_copy(br_peer(k), br_peer(k)).wait_recv()

    gain = gg[0]
    for e in range(1, B):
        gain = gain + gg[e]
    gain = gain / B
    gg_avg = gain

    pair = 2

    @pl.loop(0, N // pair)
    def _(i):
        for q in range(pair):

            @pl.when(i * pair + q != me)
            def _(q=q):
                tok_copy(i * pair + q, i * pair + q).wait_recv()

        x = jnp.concatenate([tg[i * pair + q].astype(jnp.float32) for q in range(pair)], axis=0)
        inv = lax.rsqrt(jnp.mean(x * x, axis=1, keepdims=True) + 1e-05)
        normed[pl.ds(pl.multiple_of(i * pair * T, pair * T), pair * T), :] = (
            x * inv * gg_avg
        ).astype(jnp.bfloat16)

    def hid_copy(c, slot_, peer):
        return dp_copy(
            hid.at[slot_, c], hid.at[slot_, c], hid_s.at[c, peer], hid_r.at[c, slot_], peer
        )

    for c in range(C):
        loads[c][0].wait()
        loads[c][1].wait()
        x = normed[...]
        g = jnp.dot(x, wg[c], preferred_element_type=jnp.float32)
        u = jnp.dot(x, wu[c], preferred_element_type=jnp.float32)
        hid[me, c] = (g / (1.0 + jnp.exp(-g)) * u).astype(jnp.bfloat16)

        @pl.loop(1, N)
        def _(k, c=c):
            hid_copy(c, me, dp_peer(k)).start()

        if c == 0:
            slot(jnp.int32(1))
        if c == C - 1:
            slot(jnp.int32(2))

    load_wd.wait()
    acc[...] = jnp.zeros_like(acc)
    for c in range(C):

        @pl.loop(0, N)
        def _(k, c=c):
            j = dp_peer(k)

            @pl.when(k > 0)
            def _():
                hid_copy(c, j, j).wait_recv()

            acc[...] += jnp.dot(
                hid[j, c],
                wd[pl.ds(pl.multiple_of(j * F + c * ct, ct), ct), :],
                preferred_element_type=jnp.float32,
            )

        if c == 0:
            slot(jnp.int32(3))
        if c == C - 1:
            slot(jnp.int32(4))

    def ret_copy(i, peer, from_):
        return dp_copy(rs.at[i], ret.at[from_], ret_s.at[i], ret_r.at[from_], peer)

    @pl.loop(0, N)
    def _(i):
        rs[i] = acc[pl.ds(pl.multiple_of(i * T, T), T), :].astype(jnp.bfloat16)

    @pl.loop(1, N)
    def _(k):
        ret_copy(dp_peer(k), dp_peer(k), me).start()

    ret[me] = rs[me]
    row = jnp.sum(jnp.where(routes[...] == b, route_weights[...], 0.0), axis=0, keepdims=True)
    diagonal = lax.broadcasted_iota(jnp.int32, (T, T), 0) == lax.broadcasted_iota(
        jnp.int32, (T, T), 1
    )
    weight = jnp.sum(jnp.where(diagonal, row, 0.0), axis=1, keepdims=True)

    @pl.loop(0, N)
    def _(k):
        j = dp_peer(k)

        @pl.when(k > 0)
        def _():
            ret_copy(j, j, j).wait_recv()

        part[b, j] = (ret[j].astype(jnp.float32) * weight).astype(jnp.bfloat16)

    def part_copy(e, peer):
        return br_copy(part.at[e], part.at[e], part_s.at[peer], part_r.at[e], peer)

    @pl.loop(1, B)
    def _(k):
        part_copy(b, br_peer(k)).start()

    @pl.loop(1, B)
    def _(k):
        part_copy(br_peer(k), br_peer(k)).wait_recv()

    @pl.loop(0, N)
    def _(j):
        total = part[0, j].astype(jnp.float32)
        for e in range(1, B):
            total = total + part[e, j].astype(jnp.float32)
        moe_out[j] = total

    @pl.loop(5, steps + B)
    def _(p):
        slot(p)

    for way in range(2):

        @pl.when(place[way] == 0)
        def _(way=way):
            flow[way, b] = jnp.zeros_like(flow[way, b])

        @pl.when(place[way] > 0)
        def _(way=way):
            for c in range(CHUNKS):
                kv_copy(way, b, c).wait_recv()

    for c in range(CHUNKS):
        total = (
            own(b, c).astype(jnp.float32)
            + flow[0, b, c].astype(jnp.float32)
            + flow[1, b, c].astype(jnp.float32)
        )
        kv_out[pl.ds(c * crows, crows), :] = (total / B).astype(jnp.bfloat16)

    for way in range(2):
        last = jnp.where(place[way] == 0, steps + B, steps + B - 1 - place[way])

        @pl.loop(0, steps)
        def _(s, way=way, last=last):
            @pl.when(s > last - 2)
            def _():
                sent(way, s)

    @pl.loop(1, B)
    def _(k):
        gain_copy(b, br_peer(k)).wait_send()
        part_copy(b, br_peer(k)).wait_send()

    @pl.loop(1, N)
    def _(k):
        tok_copy(me, dp_peer(k)).wait_send()
        ret_copy(dp_peer(k), dp_peer(k), me).wait_send()
        for c in range(C):
            hid_copy(c, me, dp_peer(k)).wait_send()


def local(tokens, routes, route_weights, norm_gains, keyval, gate, up, down):
    B, N = lax.axis_size("branch"), lax.axis_size("dp")
    T, D = tokens.shape
    F = gate.shape[2]
    ct = min(512, F)
    C = F // ct
    rows, wide = keyval.shape[1:]
    bw = wide // B
    H, bc = down.shape[1:]
    bf, f32 = jnp.bfloat16, jnp.float32
    dma = pltpu.SemaphoreType.DMA
    vmem, anys = pl.BlockSpec(memory_space=pltpu.VMEM), pl.BlockSpec(memory_space=pl.ANY)
    moe, merged = pl.pallas_call(
        functools.partial(kernel, B, N),
        out_shape=(
            jax.ShapeDtypeStruct((N, T, bc), f32),
            jax.ShapeDtypeStruct((rows, bw), bf),
        ),
        in_specs=[vmem] * 4 + [anys] * 4,
        out_specs=(vmem, vmem),
        scratch_shapes=[
            pltpu.VMEM((N, T, D), bf),
            pltpu.VMEM((B, 1, D), f32),
            pltpu.VMEM((N * T, D), bf),
            pltpu.VMEM((C, D, ct), bf),
            pltpu.VMEM((C, D, ct), bf),
            pltpu.VMEM((H, bc), bf),
            pltpu.VMEM((rows, wide), bf),
            pltpu.VMEM((2, B, CHUNKS, rows // CHUNKS, bw), bf),
            pltpu.VMEM((N, C, N * T, ct), bf),
            pltpu.VMEM((N * T, bc), f32),
            pltpu.VMEM((N, T, bc), bf),
            pltpu.VMEM((N, T, bc), bf),
            pltpu.VMEM((B, N, T, bc), bf),
            dma((N,)),
            dma((N,)),
            dma((B,)),
            dma((B,)),
            dma((C, N)),
            dma((C, N)),
            dma((N,)),
            dma((N,)),
            dma((B,)),
            dma((B,)),
            dma((2, B, CHUNKS)),
            dma((2, B, CHUNKS)),
            dma((C,)),
            dma((C,)),
            dma,
            dma,
        ],
        compiler_params=pltpu.CompilerParams(
            collective_id=0, has_side_effects=True, vmem_limit_bytes=56 * 2**20
        ),
    )(tokens, routes.T, route_weights.T, norm_gains, keyval, gate, up, down)
    moe = jnp.transpose(moe, (1, 0, 2)).reshape(T, D)
    return (tokens.astype(f32) + moe).astype(bf), merged


def solution(mesh):
    in_specs = (
        P("dp", None),
        P("dp", None),
        P("dp", None),
        P("branch", None),
        P("branch", "dp", None),
        P("branch", None, "dp"),
        P("branch", None, "dp"),
        P("branch", None, "dp"),
    )
    out_specs = (P("dp", None), P("dp", "branch"))
    return jax.shard_map(local, mesh=mesh, in_specs=in_specs, out_specs=out_specs, check_vma=False)
```
